512 devices in a mesh: fsdp: 64 (over x, y, z_lo), node: 8 (over z_hi, core).
Axes of the slice: x: 4, y: 4, z: 16 (z_hi: 4, z_lo: 4; z = z_hi * 4 + z_lo), core: 2. Of those that a mesh axis runs over, the one named last changes fastest.
Arguments:
- tokens: bfloat16 [24576, 4096], P('fsdp'), may hold values from -16 to 16
- norm_gain: bfloat16 [4096], replicated, may hold values from 0.5 to 1.5
- kv_cotangent: bfloat16 [24576, 2048], P('fsdp', 'node'), may hold values from -6 to 6
- weight_codes: bfloat16 [8, 4096, 256], P('node', 'fsdp'), may hold values from -127 to 127, as said below
- block_scales: bfloat16 [8, 4096], P('node', 'fsdp'), may hold values from 6.9618225e-05 to 0.0006980896
Outputs:
- d_tokens: bfloat16 [24576, 4096], P(('fsdp', 'node'))
- gain_grad: float32 [4096], replicated
- weight_grads: float32 [8, 4096, 256], P('node', 'fsdp')
The draws below stay inside these ranges and needn't reach their ends.
Inputs may be any that keep to these rules, and one draw needn't show every extreme that they name: weight_codes holds whole numbers.
All inputs are finite; a program needn't handle non-finite values.
Results may differ from the reference program's by a relative error of at most 0.018.
Values may be sent and summed in bfloat16 or wider, within the bound.
A program may use at most 64 MiB of HBM per device.

```python
import math
import jax
import jax.numpy as jnp
from jax import lax

D = 4096
HEAD = 128
BLOCK = 256
KVH = 8
TOKENS = 24576
ROWS = 4096


def draw_weight_codes(key, part):
    key = jax.random.fold_in(key, 7)
    values = jax.random.randint(key, (KVH, ROWS, BLOCK), -127, 128).astype(jnp.float32)
    values = values.at[0, 0, 0].set(-127.0).at[0, 0, 1].set(127.0)
    return values.astype(jnp.bfloat16)


def with_spikes(array, own_key, source, target, shards_of, factor):
    def block_of(axis_at):
        return (jnp.arange(array.shape[axis_at]) // (array.shape[axis_at] // shards_of)).reshape((-1,) + (1,) * (array.ndim - 1 - axis_at))

    near = jax.random.permutation(own_key, shards_of)[block_of(target)]
    other_side = (block_of(target) + shards_of // 2) % shards_of
    return jnp.where((block_of(source) == near) | (block_of(source) == other_side), factor * array, array)


def levels(stream_key, shape, split, smallest, largest):
    def one(dim, parts):
        heights = jax.random.uniform(jax.random.fold_in(jax.random.fold_in(stream_key, 6), dim), (parts,), jnp.float32, smallest / len(split), largest / len(split))
        return jnp.repeat(jnp.exp(heights), shape[dim] // parts).reshape((-1,) + (1,) * (len(shape) - dim - 1))

    gain = one(*split[0])
    for cut in split[1:]:
        gain = gain * one(*cut)
    return gain


def centred(stream_key, dims, deviation, most, split=(), held_as=jnp.bfloat16):
    entries = jax.random.normal(stream_key, dims, jnp.float32) * deviation
    if len(split) > 0:
        entries = levels(stream_key, dims, split, -0.22, 0.18) * entries
    return jnp.clip(entries, min=-most, max=most).astype(held_as)


def noise_with(key, shape, scale, most, pieces, heavy, dtype=jnp.bfloat16):
    array = scale * jax.random.normal(key, shape, jnp.float32)
    if pieces:
        array = array * levels(key, shape, pieces, -0.22, 0.18)
    return jnp.clip(with_spikes(array, jax.random.fold_in(key, 3), *heavy), -most, most).astype(dtype)


def setup_inputs(seed: int = 0) -> dict:
    streams_of = jax.random.split(jax.random.key(seed), 6)
    tokens = noise_with(streams_of[0], (TOKENS, D), 1.0, 16.0, ((0, 64),), (0, 1, 64, 4.0))
    norm_gain = jnp.clip(1.0 + 0.1 * jax.random.normal(streams_of[1], (D,), jnp.float32), 0.5, 1.5).astype(jnp.bfloat16)
    kv_cotangent = centred(streams_of[2], (TOKENS, KVH * 2 * HEAD), 1.0, 6.0, ((0, 64), (1, 8)))
    weight_codes = draw_weight_codes(jax.random.fold_in(streams_of[5], 71), 0)
    block_scales = jnp.clip(jnp.exp(math.log(0.0006980896) - 2.305321 * jax.random.uniform(streams_of[4], (KVH, ROWS), jnp.float32) ** levels(streams_of[4], (KVH, ROWS), ((0, 8), (1, 64)), -0.2, 0.2)), 6.961822509765625e-05, 0.0006980896).astype(jnp.bfloat16)
    return {"tokens": tokens, "norm_gain": norm_gain, "kv_cotangent": kv_cotangent, "weight_codes": weight_codes, "block_scales": block_scales}


def reference(tokens, norm_gain, kv_cotangent, weight_codes, block_scales):
    weights = (weight_codes.astype(jnp.float32) * block_scales.astype(jnp.float32)[:, :, None]).astype(jnp.bfloat16)
    weights = weights.reshape(KVH, D, 2 * HEAD)
    tok_float = tokens.astype(jnp.float32)
    inv_root = lax.rsqrt(lax.optimization_barrier(jnp.mean(tok_float * tok_float, axis=-1, keepdims=True)) + 1e-05)
    x_hat = tok_float * inv_root
    gain_float = norm_gain.astype(jnp.float32)
    x_norm = (x_hat * gain_float).astype(jnp.bfloat16)
    heads_first = jnp.transpose(kv_cotangent.reshape(TOKENS, KVH, 2 * HEAD), (1, 0, 2))

    def per_head(total, pair):
        cot_head, weight_head = pair
        partial_value = jnp.dot(cot_head, weight_head.T, preferred_element_type=jnp.float32).astype(jnp.bfloat16)
        partial_value = lax.optimization_barrier(partial_value)
        grad_head = lax.dot_general(x_norm, cot_head, (((0,), (0,)), ((), ())), preferred_element_type=jnp.float32)
        return (total + partial_value.astype(jnp.float32), grad_head)
    start = jnp.zeros((TOKENS, D), jnp.float32)
    d_norm, grads = lax.scan(per_head, start, (heads_first, weights))
    gain_grad = lax.optimization_barrier(jnp.sum(d_norm * x_hat, axis=0))
    scaled = gain_float * d_norm
    stat = lax.optimization_barrier(jnp.mean(scaled * x_hat, axis=-1, keepdims=True))
    d_tokens = (inv_root * (scaled - x_hat * stat)).astype(jnp.bfloat16)
    return (d_tokens, gain_grad, grads.reshape(KVH, ROWS, BLOCK))
```

```python
import jax
import jax.numpy as jnp
from jax import lax
from jax.experimental import pallas as pl
from jax.experimental.pallas import tpu as pltpu
from jax.sharding import PartitionSpec as P

MESH = pl.DeviceIdType.MESH
F32 = jnp.float32
BF16 = jnp.bfloat16
ORDER = (2, 1, 3, 0)


def kernel(
    tok_hbm, gain_ref, kv_hbm, codes_ref, scales_ref,
    dt_ref, gg_ref, wg_ref,
    cot, wbuf, tok_v, xhat, root, xs, xall, xn, xt,
    dn, dsend, drecv, dout, din,
    gs, gr, s_own, ss, sr,
    g_own, g_sib, g_z, g_xy,
    tok_sem, own_sem, za_s, za_r, w_s, w_r, x_s, x_r, xb_s, xb_r,
    c_s, c_r, g_s, g_r, q_s, q_r, e_s, e_r, a_s, a_r,
    gb_s, gb_r, gz_s, gz_r, gx_s, gx_r,
):
    fs, nd = lax.axis_index("fsdp"), lax.axis_index("node")
    zl, p = lax.rem(fs, 4), lax.div(fs, 4)
    x, y = lax.div(p, 4), lax.rem(p, 4)
    zh, c = lax.div(nd, 2), lax.rem(nd, 2)
    z = zh * 4 + zl

    def plane(xx, yy):
        return ((xx * 4 + yy) * 4 + zl, nd)

    def column(zz):
        return (p * 4 + lax.rem(zz, 4), lax.div(zz, 4) * 2 + c)

    sibling = (fs, zh * 2 + (1 - c))

    def send(src, dst, send_sem, recv_sem, device):
        pltpu.make_async_remote_copy(
            src_ref=src, dst_ref=dst, send_sem=send_sem, recv_sem=recv_sem,
            device_id=device, device_id_type=MESH,
        ).start()

    def wait(ref, sem):
        pltpu.make_async_copy(ref, ref, sem).wait()

    tok_copy = pltpu.make_async_copy(
        tok_hbm.at[pl.ds(pl.multiple_of(nd * 48, 16), 48)], tok_v, tok_sem
    )
    tok_copy.start()
    own_copy = pltpu.make_async_copy(
        kv_hbm.at[pl.ds(pl.multiple_of(zh * 96, 16), 96)], cot.at[0, x, y], own_sem
    )
    own_copy.start()

    barrier = pltpu.get_barrier_semaphore()

    def greet(o, carry):
        there = plane(lax.rem(x + lax.div(o, 4), 4), lax.rem(y + lax.rem(o, 4), 4))
        pl.semaphore_signal(barrier, inc=1, device_id=there, device_id_type=MESH)
        there = column(lax.rem(z + o, 16))
        pl.semaphore_signal(barrier, inc=1, device_id=there, device_id_type=MESH)
        return carry

    lax.fori_loop(1, 16, greet, 0)
    pl.semaphore_signal(barrier, inc=1, device_id=sibling, device_id_type=MESH)

    rows = lax.broadcasted_iota(jnp.int32, (64, 64), 0)
    cols = lax.broadcasted_iota(jnp.int32, (64, 64), 1)
    scales = jnp.broadcast_to(scales_ref[...].astype(F32), (64, 64))
    diagonal = jnp.where(rows == cols, scales, 0.0).astype(BF16)
    wbuf[z] = jnp.dot(diagonal, codes_ref[0], preferred_element_type=F32).astype(BF16)

    pl.semaphore_wait(barrier, 31)

    def share(t):
        there = lax.rem(zh + t, 4)
        slot = (4 - t) % 4
        send(
            kv_hbm.at[pl.ds(pl.multiple_of(there * 96, 16), 96)], cot.at[slot, x, y],
            za_s.at[t - 1], za_r.at[slot - 1], (fs, there * 2 + c),
        )

    def w_slot(o):
        return wbuf.at[lax.rem(z + o + 16, 16)]

    def w_send(s):
        send(w_slot(-s), w_slot(-s), w_s.at[s], w_r.at[s], column(lax.rem(z + 1, 16)))
        if s < 7:
            send(w_slot(s), w_slot(s), w_s.at[8 + s], w_r.at[8 + s], column(lax.rem(z + 15, 16)))

    def w_wait(s):
        wait(w_slot(-1 - s), w_r.at[s])
        if s < 7:
            wait(w_slot(1 + s), w_r.at[8 + s])

    share(2)
    w_send(0)
    share(1)
    share(3)

    tok_copy.wait()
    for b in range(3):
        part = pl.ds(16 * b, 16)
        t = tok_v[part].astype(F32)
        inv = lax.rsqrt(jnp.mean(t * t, axis=-1, keepdims=True) + 1e-05)
        hat = t * inv
        xhat[part] = hat
        root[part] = jnp.broadcast_to(inv, (16, 128))
        for q in range(16):
            xs[q, part] = hat[:, 256 * q : 256 * (q + 1)].astype(BF16)

    def x_push(o, carry):
        xx, yy = lax.rem(x + lax.div(o, 4), 4), lax.rem(y + lax.rem(o, 4), 4)
        send(xs.at[xx * 4 + yy], xall.at[p, c], x_s, x_r, plane(xx, yy))
        return carry

    lax.fori_loop(1, 16, x_push, 0)
    xall[p, c] = xs[p]

    def at(first, o1, o2):
        if first == 0:
            return lax.rem(x + o1 + 4, 4), lax.rem(y + o2 + 4, 4)
        return lax.rem(x + o2 + 4, 4), lax.rem(y + o1 + 4, 4)

    def one(rel, r, o):
        xx, yy = at(r, o, 0)
        return cot.at[rel, xx, yy, pl.ds(48 * r, 48)]

    def line(rel, r, o):
        xx, yy = at(r, 0, o)
        if r == 0:
            return cot.at[rel, pl.ds(0, 4), yy, pl.ds(0, 48)]
        return cot.at[rel, xx, pl.ds(0, 4), pl.ds(48, 48)]

    def push(ref, rel, r, k, o1, o2):
        send(ref, ref, c_s.at[rel, r, k], c_r.at[rel, r, k], plane(*at(r, o1, o2)))

    def stage(i, st):
        rel = ORDER[i]
        if st == 0:
            if rel:
                wait(cot.at[rel, x, y], za_r.at[rel - 1])
            else:
                own_copy.wait()
        for r in range(2):
            d = 1 if (i + r) % 2 == 0 else -1
            kd, ko = (0, 1) if d == 1 else (1, 0)
            got = lambda ref, k: wait(ref, c_r.at[rel, r, k])
            if st == 0:
                push(one(rel, r, 0), rel, r, 0, 1, 0)
                push(one(rel, r, 0), rel, r, 1, -1, 0)
            elif st == 1:
                got(one(rel, r, -d), kd)
                push(one(rel, r, -d), rel, r, 2, d, 0)
            elif st == 2:
                got(one(rel, r, d), ko)
                got(one(rel, r, 2), 2)
                push(line(rel, r, 0), rel, r, 3, 0, 1)
                push(line(rel, r, 0), rel, r, 4, 0, -1)
            elif st == 3:
                got(line(rel, r, -d), 3 + kd)
                push(line(rel, r, -d), rel, r, 5, 0, d)
            else:
                got(line(rel, r, d), 3 + ko)
                got(line(rel, r, 2), 5)

    def grads(rel):
        block = cot[rel].reshape(1536, 256)
        gs[rel] = jnp.dot(xt[...], block, preferred_element_type=F32).astype(BF16).reshape(4, 64, 256)
        for t in range(1, 4):
            there = lax.rem(zl + t, 4)
            send(gs.at[rel, there], gr.at[rel, t - 1], g_s.at[rel], g_r.at[rel], (p * 4 + there, nd))

    def near_sum(rel):
        wait(gr.at[rel], g_r.at[rel])
        total = gs[rel, zl].astype(F32)
        for t in range(3):
            total = total + gr[rel, t].astype(F32)
        if rel:
            ss[rel - 1] = total.astype(BF16)
            there = lax.rem(zh + rel, 4)
            send(ss.at[rel - 1], sr.at[rel - 1], q_s.at[rel - 1], q_r.at[rel - 1], (fs, there * 2 + c))
        else:
            s_own[...] = total

    def times_w(rel, xi):
        head = wbuf[pl.ds(lax.rem(zh + rel, 4) * 4, 4)].reshape(256, 256)
        block = cot[rel, xi].reshape(384, 256)
        return lax.dot_general(block, head, (((1,), (1,)), ((), ())), preferred_element_type=F32)

    gain_here = gain_ref[:, pl.ds(pl.multiple_of(p * 256, 256), 256)].astype(F32)

    for t in range(8):
        if t < 7:
            w_wait(t)
            w_send(t + 1)
        if t == 7:
            w_wait(7)
        for i in range(4):
            if 0 <= t - i < 5 and not (t == 7 and i == 3):
                stage(i, t - i)
        if t == 1:
            wait(xall.at[pl.ds(0, 15), 0], x_r)
            send(xall.at[pl.ds(0, 16), c], xall.at[pl.ds(0, 16), c], xb_s, xb_r, sibling)
        if t == 2:
            wait(xall.at[pl.ds(0, 16), 1 - c], xb_r)
            for q in range(16):
                xn[pl.ds(96 * q, 96)] = (xall[q].reshape(96, 256).astype(F32) * gain_here).astype(BF16)
        if t == 3:
            for q in range(12):
                xt[:, 128 * q : 128 * (q + 1)] = xn[128 * q : 128 * (q + 1)].T
        if 4 <= t < 7:
            grads(ORDER[t - 4])
        if t >= 6:
            near_sum(ORDER[t - 6])

    def three(xi, carry):
        total = times_w(2, xi) + times_w(1, xi) + times_w(3, xi)
        dn[pl.ds(4 * xi, 4)] = total.reshape(4, 2, 48, 256)
        return carry

    lax.fori_loop(0, 4, three, 0)
    stage(3, 4)

    def last(j, gain_sum):
        xi = lax.rem(x + j, 4)
        mine = pl.ds(4 * xi, 4)
        total = dn[mine] + times_w(0, xi).reshape(4, 2, 48, 256)
        dn[mine] = total
        dsend[mine] = dn[mine, 1 - c].astype(BF16)
        send(dsend.at[mine], drecv.at[mine], e_s.at[j], e_r.at[j], sibling)
        products = (total * xall[mine].astype(F32)).reshape(384, 256)
        return gain_sum + jnp.sum(products, axis=0, keepdims=True)

    g_own[...] = lax.fori_loop(0, 4, last, jnp.zeros((1, 256), F32))
    send(g_own, g_sib, gb_s, gb_r, sibling)
    grads(0)

    def turn(j, carry):
        xi = lax.rem(x + j, 4)
        mine = pl.ds(4 * xi, 4)
        wait(drecv.at[mine], e_r.at[j])
        dout[mine] = (dn[mine, c] + drecv[mine].astype(F32)).astype(BF16)

        def spread(o, inner):
            yy = lax.rem(y + o, 4)

            @pl.when(j * 4 + o > 0)
            def _():
                send(dout.at[xi * 4 + yy], din.at[p], a_s, a_r, plane(xi, yy))

            return inner

        return lax.fori_loop(0, 4, spread, carry)

    lax.fori_loop(0, 4, turn, 0)
    din[p] = dout[p]

    wait(g_sib, gb_r)
    g_z[z] = g_own[...] + g_sib[...]

    def g_push(o, carry):
        send(g_z.at[z], g_z.at[z], gz_s, gz_r, column(lax.rem(z + o, 16)))
        return carry

    lax.fori_loop(1, 16, g_push, 0)
    near_sum(3)
    near_sum(0)

    wait(g_z.at[pl.ds(0, 15)], gz_r)
    g_xy[p] = jnp.sum(g_z[...], axis=0)

    def g_spread(o, carry):
        xx, yy = lax.rem(x + lax.div(o, 4), 4), lax.rem(y + lax.rem(o, 4), 4)
        send(g_xy.at[p], g_xy.at[p], gx_s, gx_r, plane(xx, yy))
        return carry

    lax.fori_loop(1, 16, g_spread, 0)

    wait(din.at[pl.ds(0, 15)], a_r)
    gain_all = gain_ref[...].astype(F32)
    for b in range(3):
        part = pl.ds(16 * b, 16)
        d = jnp.concatenate([din[q, part] for q in range(16)], axis=1).astype(F32)
        scaled = gain_all * d
        hat = xhat[part]
        stat = jnp.mean(scaled * hat, axis=-1, keepdims=True)
        dt_ref[part] = (root[part, 0:1] * (scaled - hat * stat)).astype(BF16)

    total = s_own[...]
    for k in range(3):
        wait(sr.at[k], q_r.at[k])
        total = total + sr[k].astype(F32)
    wg_ref[...] = total

    wait(g_xy.at[pl.ds(0, 15)], gx_r)
    gg_ref[...] = g_xy[...]

    for t in range(3):
        wait(cot.at[0, 0, 0], za_s.at[t])
        wait(ss.at[t], q_s.at[t])
    for s in range(15):
        wait(wbuf.at[0], w_s.at[s])
    wait(xs.at[pl.ds(0, 15)], x_s)
    wait(xall.at[pl.ds(0, 16), 0], xb_s)
    for rel in range(4):
        for r in range(2):
            for k in range(6):
                wait(one(rel, r, 0) if k < 3 else line(rel, r, 0), c_s.at[rel, r, k])
        wait(gr.at[rel], g_s.at[rel])
        wait(dsend.at[pl.ds(0, 4)], e_s.at[rel])
    wait(dout.at[pl.ds(0, 15)], a_s)
    wait(g_own, gb_s)
    wait(g_z.at[pl.ds(0, 15)], gz_s)
    wait(g_xy.at[pl.ds(0, 15)], gx_s)


def local(tokens, norm_gain, kv_cotangent, weight_codes, block_scales):
    vmem, dma = pltpu.VMEM, pltpu.SemaphoreType.DMA
    any_spec, vmem_spec = pl.BlockSpec(memory_space=pl.ANY), pl.BlockSpec(memory_space=pltpu.VMEM)
    d_tokens, gain_grad, grads = pl.pallas_call(
        kernel,
        out_shape=(
            jax.ShapeDtypeStruct((48, 4096), BF16),
            jax.ShapeDtypeStruct((16, 1, 256), F32),
            jax.ShapeDtypeStruct((64, 256), F32),
        ),
        in_specs=[any_spec, vmem_spec, any_spec, vmem_spec, vmem_spec],
        out_specs=[vmem_spec] * 3,
        scratch_shapes=[
            vmem((4, 4, 4, 96, 256), BF16),
            vmem((16, 64, 256), BF16),
            vmem((48, 4096), BF16),
            vmem((48, 4096), F32),
            vmem((48, 128), F32),
            vmem((16, 48, 256), BF16),
            vmem((16, 2, 48, 256), BF16),
            vmem((1536, 256), BF16),
            vmem((256, 1536), BF16),
            vmem((16, 2, 48, 256), F32),
            vmem((16, 48, 256), BF16),
            vmem((16, 48, 256), BF16),
            vmem((16, 48, 256), BF16),
            vmem((16, 48, 256), BF16),
            vmem((4, 4, 64, 256), BF16),
            vmem((4, 3, 64, 256), BF16),
            vmem((64, 256), F32),
            vmem((3, 64, 256), BF16),
            vmem((3, 64, 256), BF16),
            vmem((1, 256), F32),
            vmem((1, 256), F32),
            vmem((16, 1, 256), F32),
            vmem((16, 1, 256), F32),
            dma, dma,
            dma((3,)), dma((3,)),
            dma((15,)), dma((15,)),
            dma, dma, dma, dma,
            dma((4, 2, 6)), dma((4, 2, 6)),
            dma((4,)), dma((4,)),
            dma((3,)), dma((3,)),
            dma((4,)), dma((4,)),
            dma, dma, dma, dma, dma, dma, dma, dma,
        ],
        compiler_params=pltpu.CompilerParams(
            collective_id=0, has_side_effects=True, vmem_limit_bytes=40 * 1024 * 1024
        ),
    )(tokens, norm_gain.reshape(1, 4096), kv_cotangent, weight_codes, block_scales)
    return d_tokens, gain_grad.reshape(4096), grads.reshape(1, 64, 256)


def solution(mesh):
    placed = (P("fsdp", None), P(), P("fsdp", "node"), P("node", "fsdp", None), P("node", "fsdp"))
    return jax.shard_map(
        local,
        mesh=mesh,
        in_specs=placed,
        out_specs=(P(("fsdp", "node"), None), P(), P("node", "fsdp", None)),
        check_vma=False,
    )
```

```python
import jax
import jax.numpy as jnp
from jax import lax
from jax.experimental import pallas as pl
from jax.experimental.pallas import tpu as pltpu
from jax.sharding import PartitionSpec as P

MESH = pl.DeviceIdType.MESH
F32 = jnp.float32
BF16 = jnp.bfloat16
W_GOT = ((), (-1, -2, 1, 2), (-3, -4, 3, 4), (-5, -6, 5, 6), (-7, -8, 7))
ORDER = (0, 1, 3, 2)


def kernel(
    tok_hbm, gain_ref, kv_hbm, codes_hbm, scales_hbm,
    dt_ref, gg_ref, wg_ref,
    codes_ref, scales_ref, cot, wbuf, tok_v, xhat, root, xs, xall, xn, xt,
    dn, dsend, drecv, dout, din,
    gs, gr, s_own, ss, sr,
    g_z, g_xy,
    code_sem, scale_sem, tok_sem, own_sem, za_s, za_r, w_s, w_r, x_s, x_r, xb_s, xb_r,
    c_s, c_r, g_s, g_r, q_s, q_r, e_s, e_r, a_s, a_r,
    gz_s, gz_r, gx_s, gx_r,
):
    fs, nd = lax.axis_index("fsdp"), lax.axis_index("node")
    zl, p = lax.rem(fs, 4), lax.div(fs, 4)
    x, y = lax.div(p, 4), lax.rem(p, 4)
    zh, c = lax.div(nd, 2), lax.rem(nd, 2)
    z = zh * 4 + zl

    def plane(xx, yy):
        return ((xx * 4 + yy) * 4 + zl, nd)

    def column(zz, core=c):
        return (p * 4 + lax.rem(zz, 4), lax.div(zz, 4) * 2 + core)

    sibling = (fs, zh * 2 + (1 - c))

    def send(src, dst, send_sem, recv_sem, device):
        pltpu.make_async_remote_copy(
            src_ref=src, dst_ref=dst, send_sem=send_sem, recv_sem=recv_sem,
            device_id=device, device_id_type=MESH,
        ).start()

    def wait(ref, sem):
        pltpu.make_async_copy(ref, ref, sem).wait()

    tok_copy = pltpu.make_async_copy(
        tok_hbm.at[pl.ds(pl.multiple_of(nd * 48, 16), 48)], tok_v, tok_sem
    )
    code_copy = pltpu.make_async_copy(codes_hbm, codes_ref, code_sem)
    scale_copy = pltpu.make_async_copy(scales_hbm, scales_ref, scale_sem)
    code_copy.start()
    scale_copy.start()
    tok_copy.start()
    own_copy = pltpu.make_async_copy(
        kv_hbm.at[pl.ds(pl.multiple_of(zh * 96, 16), 96)], cot.at[0, x, y], own_sem
    )
    own_copy.start()

    barrier = pltpu.get_barrier_semaphore()

    def column_any(o):
        return column(lax.rem(z + lax.div(o, 2), 16), lax.rem(c + o, 2))

    def greet_column(o, carry):
        pl.semaphore_signal(barrier, inc=1, device_id=column_any(lax.rem(o + 15, 32)), device_id_type=MESH)
        return carry

    def greet_plane(o, carry):
        there = plane(lax.rem(x + lax.div(o, 4), 4), lax.rem(y + lax.rem(o, 4), 4))
        pl.semaphore_signal(barrier, inc=1, device_id=there, device_id_type=MESH)
        return carry

    lax.fori_loop(0, 17, greet_column, 0)
    lax.fori_loop(18, 32, greet_column, 0)
    lax.fori_loop(1, 16, greet_plane, 0)

    code_copy.wait()
    scale_copy.wait()
    rows = lax.broadcasted_iota(jnp.int32, (64, 64), 0)
    cols = lax.broadcasted_iota(jnp.int32, (64, 64), 1)
    scales = jnp.broadcast_to(scales_ref[...].astype(F32), (64, 64))
    diagonal = jnp.where(rows == cols, scales, 0.0).astype(BF16)
    wbuf[z] = jnp.dot(diagonal, codes_ref[0], preferred_element_type=F32).astype(BF16)

    tok_copy.wait()
    for b in range(3):
        part = pl.ds(16 * b, 16)
        t = tok_v[part].astype(F32)
        inv = lax.rsqrt(jnp.mean(t * t, axis=-1, keepdims=True) + 1e-05)
        hat = t * inv
        xhat[part] = hat
        root[part] = jnp.broadcast_to(inv, (16, 128))
        for q in range(16):
            xs[q, part] = hat[:, 256 * q : 256 * (q + 1)].astype(BF16)
    xall[p, c] = xs[p]

    pl.semaphore_wait(barrier, 46)

    def share(t):
        there = lax.rem(zh + t, 4)
        slot = (4 - t) % 4
        for r in range(2):
            send(
                kv_hbm.at[pl.ds(pl.multiple_of(there * 96 + 48 * r, 16), 48)],
                cot.at[slot, x, y, pl.ds(48 * r, 48)],
                za_s.at[t - 1, r], za_r.at[slot - 1, r], (fs, there * 2 + c),
            )

    def w_slot(o):
        return wbuf.at[lax.rem(z + o + 16, 16)]

    def w_index(o):
        return -o - 1 if o < 0 else 7 + o

    def w_push(o, t):
        k = w_index(o - t)
        send(w_slot(o), w_slot(o), w_s.at[k], w_r.at[k], column(lax.rem(z + t + 16, 16)))

    def w_round(n):
        for o in W_GOT[n]:
            wait(w_slot(o), w_r.at[w_index(o)])
        if n == 0:
            for t in (1, -1, 2, -2):
                w_push(0, t)
        elif n < 4:
            for o in W_GOT[n]:
                if o != 6:
                    w_push(o, 2 if o < 0 else -2)

    def x_push(o, carry):
        xx, yy = lax.rem(x + lax.div(o, 4), 4), lax.rem(y + lax.rem(o, 4), 4)
        send(xs.at[xx * 4 + yy], xall.at[p, c], x_s, x_r, plane(xx, yy))
        return carry

    def at(first, o1, o2):
        if first == 0:
            return lax.rem(x + o1 + 4, 4), lax.rem(y + o2 + 4, 4)
        return lax.rem(x + o2 + 4, 4), lax.rem(y + o1 + 4, 4)

    def one(rel, r, o):
        xx, yy = at(r, o, 0)
        return cot.at[rel, xx, yy, pl.ds(48 * r, 48)]

    def line(rel, r, o):
        xx, yy = at(r, 0, o)
        if r == 0:
            return cot.at[rel, pl.ds(0, 4), yy, pl.ds(0, 48)]
        return cot.at[rel, xx, pl.ds(0, 4), pl.ds(48, 48)]

    def push(ref, rel, r, k, o1, o2):
        send(ref, ref, c_s.at[rel, r, k], c_r.at[rel, r, k], plane(*at(r, o1, o2)))

    def stage(i, st):
        rel, direct = ORDER[i], i == 3
        if st == 0 and not rel:
            own_copy.wait()
        for r in range(2):
            d = 1 if (i + r) % 2 == 0 else -1
            kd, ko = (3, 4) if d == 1 else (4, 3)
            got = lambda ref, k: wait(ref, c_r.at[rel, r, k])
            if st == 0:
                if rel:
                    wait(one(rel, r, 0), za_r.at[rel - 1, r])
                push(one(rel, r, 0), rel, r, 2, 2, 0)
                push(one(rel, r, 0), rel, r, 0, 1, 0)
                push(one(rel, r, 0), rel, r, 1, -1, 0)
            elif st == 1:
                got(one(rel, r, -1), 0)
                got(one(rel, r, 1), 1)
                got(one(rel, r, 2), 2)
                if direct:
                    push(line(rel, r, 0), rel, r, 5, 0, 2)
                push(line(rel, r, 0), rel, r, 3, 0, 1)
                push(line(rel, r, 0), rel, r, 4, 0, -1)
            elif st == 2:
                got(line(rel, r, -d), kd)
                if not direct:
                    push(line(rel, r, -d), rel, r, 5, 0, d)
            else:
                got(line(rel, r, d), ko)
                got(line(rel, r, 2), 5)

    def grads(rel):
        block = cot[rel].reshape(1536, 256)
        gs[rel] = jnp.dot(xt[...], block, preferred_element_type=F32).astype(BF16).reshape(4, 64, 256)
        for t in range(1, 4):
            there = lax.rem(zl + t, 4)
            send(gs.at[rel, there], gr.at[rel, t - 1], g_s.at[rel], g_r.at[rel], (p * 4 + there, nd))

    def near_sum(rel):
        wait(gr.at[rel], g_r.at[rel])
        total = gs[rel, zl].astype(F32)
        for t in range(3):
            total = total + gr[rel, t].astype(F32)
        if rel:
            ss[rel - 1] = total.astype(BF16)
            there = lax.rem(zh + rel, 4)
            send(ss.at[rel - 1], sr.at[rel - 1], q_s.at[rel - 1], q_r.at[rel - 1], (fs, there * 2 + c))
        else:
            s_own[...] = total

    def times_w(rel, xi):
        head = wbuf[pl.ds(lax.rem(zh + rel, 4) * 4, 4)].reshape(256, 256)
        block = cot[rel, xi].reshape(384, 256)
        return lax.dot_general(block, head, (((1,), (1,)), ((), ())), preferred_element_type=F32)

    gain_here = gain_ref[:, pl.ds(pl.multiple_of(p * 256, 256), 256)].astype(F32)

    share(1)
    share(3)
    stage(0, 0)
    lax.fori_loop(1, 16, x_push, 0)
    stage(0, 1)
    w_round(0)
    share(2)
    stage(1, 0)
    stage(2, 0)
    stage(0, 2)
    wait(xall.at[pl.ds(0, 15), 0], x_r)
    send(xall.at[pl.ds(0, 16), c], xall.at[pl.ds(0, 16), c], xb_s, xb_r, sibling)
    w_round(1)
    stage(1, 1)
    stage(2, 1)
    stage(3, 0)
    stage(0, 3)
    wait(xall.at[pl.ds(0, 16), 1 - c], xb_r)
    for q in range(16):
        xn[pl.ds(96 * q, 96)] = (xall[q].reshape(96, 256).astype(F32) * gain_here).astype(BF16)
    for q in range(12):
        xt[:, 128 * q : 128 * (q + 1)] = xn[128 * q : 128 * (q + 1)].T
    w_round(2)
    stage(1, 2)
    stage(2, 2)
    grads(ORDER[0])
    stage(3, 1)
    w_round(3)
    stage(1, 3)
    grads(ORDER[1])
    stage(2, 3)
    grads(ORDER[2])
    near_sum(ORDER[0])
    w_round(4)

    def three(xi, carry):
        total = times_w(ORDER[0], xi) + times_w(ORDER[1], xi) + times_w(ORDER[2], xi)
        dn[pl.ds(4 * xi, 4)] = total.reshape(4, 2, 48, 256)
        return carry

    lax.fori_loop(0, 4, three, 0)
    near_sum(ORDER[1])
    near_sum(ORDER[2])
    stage(3, 2)
    stage(3, 3)

    def last(j, gain_sum):
        xi = lax.rem(x + j, 4)
        mine = pl.ds(4 * xi, 4)
        total = dn[mine] + times_w(ORDER[3], xi).reshape(4, 2, 48, 256)
        dn[mine] = total
        dsend[mine] = dn[mine, 1 - c].astype(BF16)
        send(dsend.at[mine], drecv.at[mine], e_s.at[j], e_r.at[j], sibling)
        products = (total * xall[mine].astype(F32)).reshape(384, 256)
        return gain_sum + jnp.sum(products, axis=0, keepdims=True)

    g_z[z * 2 + c] = lax.fori_loop(0, 4, last, jnp.zeros((1, 256), F32))

    def g_push(o, carry):
        send(g_z.at[z * 2 + c], g_z.at[z * 2 + c], gz_s, gz_r, column_any(lax.rem(o + 15, 32)))
        return carry

    lax.fori_loop(0, 17, g_push, 0)
    lax.fori_loop(18, 32, g_push, 0)
    grads(ORDER[3])

    def turn(j, carry):
        xi = lax.rem(x + j, 4)
        mine = pl.ds(4 * xi, 4)
        wait(drecv.at[mine], e_r.at[j])
        dout[mine] = (dn[mine, c] + drecv[mine].astype(F32)).astype(BF16)

        def spread(o, inner):
            yy = lax.rem(y + o, 4)

            @pl.when(j * 4 + o > 0)
            def _():
                send(dout.at[xi * 4 + yy], din.at[p], a_s, a_r, plane(xi, yy))

            return inner

        return lax.fori_loop(0, 4, spread, carry)

    lax.fori_loop(0, 4, turn, 0)
    din[p] = dout[p]

    near_sum(ORDER[3])

    wait(g_z.at[pl.ds(0, 31)], gz_r)
    g_xy[p] = jnp.sum(g_z[...], axis=0)

    def g_spread(o, carry):
        xx, yy = lax.rem(x + lax.div(o, 4), 4), lax.rem(y + lax.rem(o, 4), 4)
        send(g_xy.at[p], g_xy.at[p], gx_s, gx_r, plane(xx, yy))
        return carry

    lax.fori_loop(1, 16, g_spread, 0)

    wait(din.at[pl.ds(0, 15)], a_r)
    gain_all = gain_ref[...].astype(F32)
    for b in range(3):
        part = pl.ds(16 * b, 16)
        d = jnp.concatenate([din[q, part] for q in range(16)], axis=1).astype(F32)
        scaled = gain_all * d
        hat = xhat[part]
        stat = jnp.mean(scaled * hat, axis=-1, keepdims=True)
        dt_ref[part] = (root[part, 0:1] * (scaled - hat * stat)).astype(BF16)

    total = s_own[...]
    for k in range(3):
        wait(sr.at[k], q_r.at[k])
        total = total + sr[k].astype(F32)
    wg_ref[...] = total

    wait(g_xy.at[pl.ds(0, 15)], gx_r)
    gg_ref[...] = g_xy[...]

    for t in range(3):
        for r in range(2):
            wait(one(0, r, 0), za_s.at[t, r])
        wait(ss.at[t], q_s.at[t])
    for s in range(15):
        wait(wbuf.at[0], w_s.at[s])
    wait(xs.at[pl.ds(0, 15)], x_s)
    wait(xall.at[pl.ds(0, 16), 0], xb_s)
    for rel in range(4):
        for r in range(2):
            for k in range(6):
                wait(one(rel, r, 0) if k < 3 else line(rel, r, 0), c_s.at[rel, r, k])
        wait(gr.at[rel], g_s.at[rel])
        wait(dsend.at[pl.ds(0, 4)], e_s.at[rel])
    wait(dout.at[pl.ds(0, 15)], a_s)
    wait(g_z.at[pl.ds(0, 31)], gz_s)
    wait(g_xy.at[pl.ds(0, 15)], gx_s)


def local(tokens, norm_gain, kv_cotangent, weight_codes, block_scales):
    vmem, dma = pltpu.VMEM, pltpu.SemaphoreType.DMA
    hbm_spec, vmem_spec = pl.BlockSpec(memory_space=pltpu.HBM), pl.BlockSpec(memory_space=pltpu.VMEM)
    d_tokens, gain_grad, grads = pl.pallas_call(
        kernel,
        out_shape=(
            jax.ShapeDtypeStruct((48, 4096), BF16),
            jax.ShapeDtypeStruct((16, 1, 256), F32),
            jax.ShapeDtypeStruct((64, 256), F32),
        ),
        in_specs=[hbm_spec, vmem_spec, hbm_spec, hbm_spec, hbm_spec],
        out_specs=[vmem_spec] * 3,
        scratch_shapes=[
            vmem((1, 64, 256), BF16),
            vmem((1, 64), BF16),
            vmem((4, 4, 4, 96, 256), BF16),
            vmem((16, 64, 256), BF16),
            vmem((48, 4096), BF16),
            vmem((48, 4096), F32),
            vmem((48, 128), F32),
            vmem((16, 48, 256), BF16),
            vmem((16, 2, 48, 256), BF16),
            vmem((1536, 256), BF16),
            vmem((256, 1536), BF16),
            vmem((16, 2, 48, 256), F32),
            vmem((16, 48, 256), BF16),
            vmem((16, 48, 256), BF16),
            vmem((16, 48, 256), BF16),
            vmem((16, 48, 256), BF16),
            vmem((4, 4, 64, 256), BF16),
            vmem((4, 3, 64, 256), BF16),
            vmem((64, 256), F32),
            vmem((3, 64, 256), BF16),
            vmem((3, 64, 256), BF16),
            vmem((32, 1, 256), F32),
            vmem((16, 1, 256), F32),
            dma, dma, dma, dma,
            dma((3, 2)), dma((3, 2)),
            dma((15,)), dma((15,)),
            dma, dma, dma, dma,
            dma((4, 2, 6)), dma((4, 2, 6)),
            dma((4,)), dma((4,)),
            dma((3,)), dma((3,)),
            dma((4,)), dma((4,)),
            dma, dma, dma, dma, dma, dma,
        ],
        compiler_params=pltpu.CompilerParams(
            collective_id=0, has_side_effects=True, vmem_limit_bytes=52 * 1024 * 1024
        ),
    )(tokens, norm_gain.reshape(1, 4096), kv_cotangent, weight_codes, block_scales)
    return d_tokens, gain_grad.reshape(4096), grads.reshape(1, 64, 256)


def solution(mesh):
    placed = (P("fsdp", None), P(), P("fsdp", "node"), P("node", "fsdp", None), P("node", "fsdp"))
    return jax.shard_map(
        local,
        mesh=mesh,
        in_specs=placed,
        out_specs=(P(("fsdp", "node"), None), P(), P("node", "fsdp", None)),
        check_vma=False,
    )
```

```python
import jax
import jax.numpy as jnp
from jax import lax
from jax.experimental import pallas as pl
from jax.experimental.pallas import tpu as pltpu
from jax.sharding import PartitionSpec as P

MESH = pl.DeviceIdType.MESH
F32 = jnp.float32
BF16 = jnp.bfloat16
W_GOT = ((), (-1, -2, 1, 2), (-3, -4, 3, 4), (-5, -6, 5, 6), (-7, -8, 7))
ORDER = (0, 1, 3, 2)


def kernel(
    tok_hbm, gain_hbm, kv_hbm, codes_hbm, scales_hbm,
    dt_ref, gg_ref, wg_ref,
    gain_ref, gain_row, codes_ref, scales_ref, cot, wbuf, tok_v, xhat, root, xs, xall, xn, xt,
    dn, dsend, drecv, dout, din,
    gs, gr, s_own, ss, sr,
    g_z, g_xy,
    gain_sem, code_sem, scale_sem, tok_sem, own_sem, za_s, za_r, w_s, w_r, x_s, x_r, xb_s, xb_r,
    c_s, c_r, g_s, g_r, q_s, q_r, e_s, e_r, a_s, a_r,
    gz_s, gz_r, gx_s, gx_r,
):
    fs, nd = lax.axis_index("fsdp"), lax.axis_index("node")
    zl, p = lax.rem(fs, 4), lax.div(fs, 4)
    x, y = lax.div(p, 4), lax.rem(p, 4)
    zh, c = lax.div(nd, 2), lax.rem(nd, 2)
    z = zh * 4 + zl

    def plane(xx, yy):
        return ((xx * 4 + yy) * 4 + zl, nd)

    def column(zz, core=c):
        return (p * 4 + lax.rem(zz, 4), lax.div(zz, 4) * 2 + core)

    sibling = (fs, zh * 2 + (1 - c))

    def send(src, dst, send_sem, recv_sem, device):
        pltpu.make_async_remote_copy(
            src_ref=src, dst_ref=dst, send_sem=send_sem, recv_sem=recv_sem,
            device_id=device, device_id_type=MESH,
        ).start()

    def wait(ref, sem):
        pltpu.make_async_copy(ref, ref, sem).wait()

    tok_copy = pltpu.make_async_copy(
        tok_hbm.at[pl.ds(pl.multiple_of(nd * 48, 16), 48)], tok_v, tok_sem
    )
    code_copy = pltpu.make_async_copy(codes_hbm, codes_ref, code_sem)
    scale_copy = pltpu.make_async_copy(scales_hbm, scales_ref, scale_sem)
    gain_copy = pltpu.make_async_copy(gain_hbm, gain_ref, gain_sem)
    code_copy.start()
    gain_copy.start()
    scale_copy.start()
    tok_copy.start()
    own_copy = pltpu.make_async_copy(
        kv_hbm.at[pl.ds(pl.multiple_of(zh * 96, 16), 96)], cot.at[0, x, y], own_sem
    )
    own_copy.start()

    barrier = pltpu.get_barrier_semaphore()

    def column_any(o):
        return column(lax.rem(z + lax.div(o, 2), 16), lax.rem(c + o, 2))

    def greet_column(o, carry):
        pl.semaphore_signal(barrier, inc=1, device_id=column_any(lax.rem(o + 15, 32)), device_id_type=MESH)
        return carry

    def greet_plane(o, carry):
        there = plane(lax.rem(x + lax.div(o, 4), 4), lax.rem(y + lax.rem(o, 4), 4))
        pl.semaphore_signal(barrier, inc=1, device_id=there, device_id_type=MESH)
        return carry

    lax.fori_loop(0, 17, greet_column, 0)
    lax.fori_loop(18, 32, greet_column, 0)
    lax.fori_loop(1, 16, greet_plane, 0)

    code_copy.wait()
    scale_copy.wait()
    rows = lax.broadcasted_iota(jnp.int32, (64, 64), 0)
    cols = lax.broadcasted_iota(jnp.int32, (64, 64), 1)
    scales = jnp.broadcast_to(scales_ref[...].astype(F32), (64, 64))
    diagonal = jnp.where(rows == cols, scales, 0.0).astype(BF16)
    wbuf[z] = jnp.dot(diagonal, codes_ref[0], preferred_element_type=F32).astype(BF16)

    tok_copy.wait()
    for b in range(3):
        part = pl.ds(16 * b, 16)
        t = tok_v[part].astype(F32)
        inv = lax.rsqrt(jnp.mean(t * t, axis=-1, keepdims=True) + 1e-05)
        hat = t * inv
        xhat[part] = hat
        root[part] = jnp.broadcast_to(inv, (16, 128))
        for q in range(16):
            xs[q, part] = hat[:, 256 * q : 256 * (q + 1)].astype(BF16)
    xall[p, c] = xs[p]

    gain_copy.wait()
    gain_row[...] = gain_ref[...].astype(F32).reshape(1, 4096)

    pl.semaphore_wait(barrier, 46)

    def share(t):
        there = lax.rem(zh + t, 4)
        slot = (4 - t) % 4
        for r in range(2):
            send(
                kv_hbm.at[pl.ds(pl.multiple_of(there * 96 + 48 * r, 16), 48)],
                cot.at[slot, x, y, pl.ds(48 * r, 48)],
                za_s.at[t - 1, r], za_r.at[slot - 1, r], (fs, there * 2 + c),
            )

    def w_slot(o):
        return wbuf.at[lax.rem(z + o + 16, 16)]

    def w_index(o):
        return -o - 1 if o < 0 else 7 + o

    def w_push(o, t):
        k = w_index(o - t)
        send(w_slot(o), w_slot(o), w_s.at[k], w_r.at[k], column(lax.rem(z + t + 16, 16)))

    def w_round(n):
        for o in W_GOT[n]:
            wait(w_slot(o), w_r.at[w_index(o)])
        if n == 0:
            for t in (1, -1, 2, -2):
                w_push(0, t)
        elif n < 4:
            for o in W_GOT[n]:
                if o != 6:
                    w_push(o, 2 if o < 0 else -2)

    def x_push(o, carry):
        xx, yy = lax.rem(x + lax.div(o, 4), 4), lax.rem(y + lax.rem(o, 4), 4)
        send(xs.at[xx * 4 + yy], xall.at[p, c], x_s, x_r, plane(xx, yy))
        return carry

    def at(first, o1, o2):
        if first == 0:
            return lax.rem(x + o1 + 4, 4), lax.rem(y + o2 + 4, 4)
        return lax.rem(x + o2 + 4, 4), lax.rem(y + o1 + 4, 4)

    def one(rel, r, o):
        xx, yy = at(r, o, 0)
        return cot.at[rel, xx, yy, pl.ds(48 * r, 48)]

    def line(rel, r, o):
        xx, yy = at(r, 0, o)
        if r == 0:
            return cot.at[rel, pl.ds(0, 4), yy, pl.ds(0, 48)]
        return cot.at[rel, xx, pl.ds(0, 4), pl.ds(48, 48)]

    def push(ref, rel, r, k, o1, o2):
        send(ref, ref, c_s.at[rel, r, k], c_r.at[rel, r, k], plane(*at(r, o1, o2)))

    def stage(i, st):
        rel, direct = ORDER[i], i == 3
        if st == 0 and not rel:
            own_copy.wait()
        for r in range(2):
            d = 1 if (i + r) % 2 == 0 else -1
            kd, ko = (3, 4) if d == 1 else (4, 3)
            got = lambda ref, k: wait(ref, c_r.at[rel, r, k])
            if st == 0:
                if rel:
                    wait(one(rel, r, 0), za_r.at[rel - 1, r])
                push(one(rel, r, 0), rel, r, 2, 2, 0)
                push(one(rel, r, 0), rel, r, 0, 1, 0)
                push(one(rel, r, 0), rel, r, 1, -1, 0)
            elif st == 1:
                got(one(rel, r, -1), 0)
                got(one(rel, r, 1), 1)
                got(one(rel, r, 2), 2)
                if direct:
                    push(line(rel, r, 0), rel, r, 5, 0, 2)
                push(line(rel, r, 0), rel, r, 3, 0, 1)
                push(line(rel, r, 0), rel, r, 4, 0, -1)
            elif st == 2:
                got(line(rel, r, -d), kd)
                if not direct:
                    push(line(rel, r, -d), rel, r, 5, 0, d)
            else:
                got(line(rel, r, d), ko)
                got(line(rel, r, 2), 5)

    def grads(rel):
        block = cot[rel].reshape(1536, 256)
        gs[rel] = jnp.dot(xt[...], block, preferred_element_type=F32).astype(BF16).reshape(4, 64, 256)
        for t in range(1, 4):
            there = lax.rem(zl + t, 4)
            send(gs.at[rel, there], gr.at[rel, t - 1], g_s.at[rel], g_r.at[rel], (p * 4 + there, nd))

    def near_sum(rel):
        wait(gr.at[rel], g_r.at[rel])
        total = gs[rel, zl].astype(F32)
        for t in range(3):
            total = total + gr[rel, t].astype(F32)
        if rel:
            ss[rel - 1] = total.astype(BF16)
            there = lax.rem(zh + rel, 4)
            send(ss.at[rel - 1], sr.at[rel - 1], q_s.at[rel - 1], q_r.at[rel - 1], (fs, there * 2 + c))
        else:
            s_own[...] = total

    def times_w(rel, xi):
        head = wbuf[pl.ds(lax.rem(zh + rel, 4) * 4, 4)].reshape(256, 256)
        block = cot[rel, xi].reshape(384, 256)
        return lax.dot_general(block, head, (((1,), (1,)), ((), ())), preferred_element_type=F32)

    gain_here = gain_row[:, pl.ds(pl.multiple_of(p * 256, 256), 256)]

    w_round(0)
    share(1)
    share(3)
    stage(0, 0)
    share(2)
    lax.fori_loop(1, 16, x_push, 0)
    stage(0, 1)
    w_round(1)
    stage(1, 0)
    stage(2, 0)
    stage(0, 2)
    w_round(2)
    stage(1, 1)
    stage(2, 1)
    stage(3, 0)
    stage(0, 3)
    wait(xall.at[pl.ds(0, 15), 0], x_r)
    send(xall.at[pl.ds(0, 16), c], xall.at[pl.ds(0, 16), c], xb_s, xb_r, sibling)
    w_round(3)
    stage(1, 2)
    stage(2, 2)
    stage(3, 1)
    wait(xall.at[pl.ds(0, 16), 1 - c], xb_r)
    for q in range(16):
        xn[pl.ds(96 * q, 96)] = (xall[q].reshape(96, 256).astype(F32) * gain_here).astype(BF16)
    for q in range(12):
        xt[:, 128 * q : 128 * (q + 1)] = xn[128 * q : 128 * (q + 1)].T
    grads(ORDER[0])
    stage(1, 3)
    grads(ORDER[1])
    stage(2, 3)
    grads(ORDER[2])
    w_round(4)

    def three(xi, carry):
        total = times_w(ORDER[0], xi) + times_w(ORDER[1], xi) + times_w(ORDER[2], xi)
        dn[pl.ds(4 * xi, 4)] = total.reshape(4, 2, 48, 256)
        return carry

    lax.fori_loop(0, 4, three, 0)
    stage(3, 2)
    stage(3, 3)

    def last(j, gain_sum):
        xi = lax.rem(x + j, 4)
        mine = pl.ds(4 * xi, 4)
        total = dn[mine] + times_w(ORDER[3], xi).reshape(4, 2, 48, 256)
        dn[mine] = total
        dsend[mine] = dn[mine, 1 - c].astype(BF16)
        send(dsend.at[mine], drecv.at[mine], e_s.at[j], e_r.at[j], sibling)
        products = (total * xall[mine].astype(F32)).reshape(384, 256)
        return gain_sum + jnp.sum(products, axis=0, keepdims=True)

    g_z[z * 2 + c] = lax.fori_loop(0, 4, last, jnp.zeros((1, 256), F32))

    def g_push(o, carry):
        send(g_z.at[z * 2 + c], g_z.at[z * 2 + c], gz_s, gz_r, column_any(lax.rem(o + 15, 32)))
        return carry

    lax.fori_loop(0, 17, g_push, 0)
    lax.fori_loop(18, 32, g_push, 0)
    grads(ORDER[3])

    def turn(j, carry):
        xi = lax.rem(x + j, 4)
        mine = pl.ds(4 * xi, 4)
        wait(drecv.at[mine], e_r.at[j])
        dout[mine] = (dn[mine, c] + drecv[mine].astype(F32)).astype(BF16)

        def spread(o, inner):
            yy = lax.rem(y + o, 4)

            @pl.when(j * 4 + o > 0)
            def _():
                send(dout.at[xi * 4 + yy], din.at[p], a_s, a_r, plane(xi, yy))

            return inner

        return lax.fori_loop(0, 4, spread, carry)

    lax.fori_loop(0, 4, turn, 0)
    din[p] = dout[p]

    near_sum(ORDER[1])
    near_sum(ORDER[2])
    near_sum(ORDER[0])
    near_sum(ORDER[3])

    wait(g_z.at[pl.ds(0, 31)], gz_r)
    g_xy[p] = jnp.sum(g_z[...], axis=0)

    def g_spread(o, carry):
        xx, yy = lax.rem(x + lax.div(o, 4), 4), lax.rem(y + lax.rem(o, 4), 4)
        send(g_xy.at[p], g_xy.at[p], gx_s, gx_r, plane(xx, yy))
        return carry

    lax.fori_loop(1, 16, g_spread, 0)

    wait(din.at[pl.ds(0, 15)], a_r)
    gain_all = gain_row[...]
    for b in range(3):
        part = pl.ds(16 * b, 16)
        d = jnp.concatenate([din[q, part] for q in range(16)], axis=1).astype(F32)
        scaled = gain_all * d
        hat = xhat[part]
        stat = jnp.mean(scaled * hat, axis=-1, keepdims=True)
        dt_ref[part] = (root[part, 0:1] * (scaled - hat * stat)).astype(BF16)

    total = s_own[...]
    for k in range(3):
        wait(sr.at[k], q_r.at[k])
        total = total + sr[k].astype(F32)
    wg_ref[...] = total

    wait(g_xy.at[pl.ds(0, 15)], gx_r)
    gg_ref[...] = g_xy[...]

    for t in range(3):
        for r in range(2):
            wait(one(0, r, 0), za_s.at[t, r])
        wait(ss.at[t], q_s.at[t])
    for s in range(15):
        wait(wbuf.at[0], w_s.at[s])
    wait(xs.at[pl.ds(0, 15)], x_s)
    wait(xall.at[pl.ds(0, 16), 0], xb_s)
    for rel in range(4):
        for r in range(2):
            for k in range(6):
                wait(one(rel, r, 0) if k < 3 else line(rel, r, 0), c_s.at[rel, r, k])
        wait(gr.at[rel], g_s.at[rel])
        wait(dsend.at[pl.ds(0, 4)], e_s.at[rel])
    wait(dout.at[pl.ds(0, 15)], a_s)
    wait(g_z.at[pl.ds(0, 31)], gz_s)
    wait(g_xy.at[pl.ds(0, 15)], gx_s)


def local(tokens, norm_gain, kv_cotangent, weight_codes, block_scales):
    vmem, dma = pltpu.VMEM, pltpu.SemaphoreType.DMA
    hbm_spec, vmem_spec = pl.BlockSpec(memory_space=pltpu.HBM), pl.BlockSpec(memory_space=pltpu.VMEM)
    d_tokens, gain_grad, grads = pl.pallas_call(
        kernel,
        out_shape=(
            jax.ShapeDtypeStruct((48, 4096), BF16),
            jax.ShapeDtypeStruct((16, 1, 256), F32),
            jax.ShapeDtypeStruct((64, 256), F32),
        ),
        in_specs=[hbm_spec] * 5,
        out_specs=[vmem_spec] * 3,
        scratch_shapes=[
            vmem((4096,), BF16),
            vmem((1, 4096), F32),
            vmem((1, 64, 256), BF16),
            vmem((1, 64), BF16),
            vmem((4, 4, 4, 96, 256), BF16),
            vmem((16, 64, 256), BF16),
            vmem((48, 4096), BF16),
            vmem((48, 4096), F32),
            vmem((48, 128), F32),
            vmem((16, 48, 256), BF16),
            vmem((16, 2, 48, 256), BF16),
            vmem((1536, 256), BF16),
            vmem((256, 1536), BF16),
            vmem((16, 2, 48, 256), F32),
            vmem((16, 48, 256), BF16),
            vmem((16, 48, 256), BF16),
            vmem((16, 48, 256), BF16),
            vmem((16, 48, 256), BF16),
            vmem((4, 4, 64, 256), BF16),
            vmem((4, 3, 64, 256), BF16),
            vmem((64, 256), F32),
            vmem((3, 64, 256), BF16),
            vmem((3, 64, 256), BF16),
            vmem((32, 1, 256), F32),
            vmem((16, 1, 256), F32),
            dma, dma, dma, dma, dma,
            dma((3, 2)), dma((3, 2)),
            dma((15,)), dma((15,)),
            dma, dma, dma, dma,
            dma((4, 2, 6)), dma((4, 2, 6)),
            dma((4,)), dma((4,)),
            dma((3,)), dma((3,)),
            dma((4,)), dma((4,)),
            dma, dma, dma, dma, dma, dma,
        ],
        compiler_params=pltpu.CompilerParams(
            collective_id=0, has_side_effects=True, vmem_limit_bytes=52 * 1024 * 1024
        ),
    )(*[pltpu.with_memory_space_constraint(a, pltpu.HBM) for a in (tokens, norm_gain, kv_cotangent, weight_codes, block_scales)])
    return d_tokens, gain_grad.reshape(4096), grads.reshape(1, 64, 256)


def solution(mesh):
    placed = (P("fsdp", None), P(), P("fsdp", "node"), P("node", "fsdp", None), P("node", "fsdp"))
    return jax.shard_map(
        local,
        mesh=mesh,
        in_specs=placed,
        out_specs=(P(("fsdp", "node"), None), P(), P("node", "fsdp", None)),
        check_vma=False,
    )
```

```python
import jax
import jax.numpy as jnp
from jax import lax
from jax.experimental import pallas as pl
from jax.experimental.pallas import tpu as pltpu
from jax.sharding import PartitionSpec as P

MESH = pl.DeviceIdType.MESH
F32 = jnp.float32
BF16 = jnp.bfloat16
W_GOT = ((), (-1, -2, 1, 2), (-3, -4, 3, 4), (-5, -6, 5, 6), (-7, -8, 7))
ORDER = (0, 1, 3, 2)


def kernel(
    tok_hbm, gain_hbm, kv_hbm, codes_hbm, scales_hbm,
    dt_ref, gg_ref, wg_ref,
    gain_ref, gain_row, codes_ref, scales_ref, cot, wbuf, tok_v, xhat, root, xs, xall, xn, xt,
    dn, dsend, drecv, dout, din,
    gs, gr, s_own, ss, sr,
    g_z, g_xy,
    gain_sem, code_sem, scale_sem, tok_sem, own_sem, za_s, za_r, w_s, w_r, x_s, x_r, xb_s, xb_r,
    c_s, c_r, g_s, g_r, q_s, q_r, e_s, e_r, a_s, a_r,
    gz_s, gz_r, gx_s, gx_r,
):
    fs, nd = lax.axis_index("fsdp"), lax.axis_index("node")
    zl, p = lax.rem(fs, 4), lax.div(fs, 4)
    x, y = lax.div(p, 4), lax.rem(p, 4)
    zh, c = lax.div(nd, 2), lax.rem(nd, 2)
    z = zh * 4 + zl

    def plane(xx, yy):
        return ((xx * 4 + yy) * 4 + zl, nd)

    def column(zz, core=c):
        return (p * 4 + lax.rem(zz, 4), lax.div(zz, 4) * 2 + core)

    sibling = (fs, zh * 2 + (1 - c))

    def send(src, dst, send_sem, recv_sem, device):
        pltpu.make_async_remote_copy(
            src_ref=src, dst_ref=dst, send_sem=send_sem, recv_sem=recv_sem,
            device_id=device, device_id_type=MESH,
        ).start()

    def wait(ref, sem):
        pltpu.make_async_copy(ref, ref, sem).wait()

    tok_copy = pltpu.make_async_copy(
        tok_hbm.at[pl.ds(pl.multiple_of(nd * 48, 16), 48)], tok_v, tok_sem
    )
    code_copy = pltpu.make_async_copy(codes_hbm, codes_ref, code_sem)
    scale_copy = pltpu.make_async_copy(scales_hbm, scales_ref, scale_sem)
    gain_copy = pltpu.make_async_copy(gain_hbm, gain_ref, gain_sem)
    code_copy.start()
    gain_copy.start()
    scale_copy.start()
    tok_copy.start()
    own_copy = pltpu.make_async_copy(
        kv_hbm.at[pl.ds(pl.multiple_of(zh * 96, 16), 96)], cot.at[0, x, y], own_sem
    )
    own_copy.start()

    barrier = pltpu.get_barrier_semaphore()

    def column_any(o):
        return column(lax.rem(z + lax.div(o, 2), 16), lax.rem(c + o, 2))

    def greet_column(o, carry):
        pl.semaphore_signal(barrier, inc=1, device_id=column_any(lax.rem(o + 15, 32)), device_id_type=MESH)
        return carry

    def greet_plane(o, carry):
        there = plane(lax.rem(x + lax.div(o, 4), 4), lax.rem(y + lax.rem(o, 4), 4))
        pl.semaphore_signal(barrier, inc=1, device_id=there, device_id_type=MESH)
        return carry

    lax.fori_loop(0, 17, greet_column, 0)
    lax.fori_loop(18, 32, greet_column, 0)
    lax.fori_loop(1, 16, greet_plane, 0)

    code_copy.wait()
    scale_copy.wait()
    rows = lax.broadcasted_iota(jnp.int32, (64, 64), 0)
    cols = lax.broadcasted_iota(jnp.int32, (64, 64), 1)
    scales = jnp.broadcast_to(scales_ref[...].astype(F32), (64, 64))
    diagonal = jnp.where(rows == cols, scales, 0.0).astype(BF16)
    wbuf[z] = jnp.dot(diagonal, codes_ref[0], preferred_element_type=F32).astype(BF16)

    tok_copy.wait()
    for b in range(3):
        part = pl.ds(16 * b, 16)
        t = tok_v[part].astype(F32)
        inv = lax.rsqrt(jnp.mean(t * t, axis=-1, keepdims=True) + 1e-05)
        hat = t * inv
        xhat[part] = hat
        root[part] = jnp.broadcast_to(inv, (16, 128))
        for q in range(16):
            xs[q, part] = hat[:, 256 * q : 256 * (q + 1)].astype(BF16)
    xall[p, c] = xs[p]

    gain_copy.wait()
    gain_row[...] = gain_ref[...].astype(F32).reshape(1, 4096)

    pl.semaphore_wait(barrier, 46)

    def share(t):
        there = lax.rem(zh + t, 4)
        slot = (4 - t) % 4
        for r in range(2):
            send(
                kv_hbm.at[pl.ds(pl.multiple_of(there * 96 + 48 * r, 16), 48)],
                cot.at[slot, x, y, pl.ds(48 * r, 48)],
                za_s.at[t - 1, r], za_r.at[slot - 1, r], (fs, there * 2 + c),
            )

    def w_slot(o):
        return wbuf.at[lax.rem(z + o + 16, 16)]

    def w_index(o):
        return -o - 1 if o < 0 else 7 + o

    def w_push(o, t):
        k = w_index(o - t)
        send(w_slot(o), w_slot(o), w_s.at[k], w_r.at[k], column(lax.rem(z + t + 16, 16)))

    def w_round(n):
        for o in W_GOT[n]:
            wait(w_slot(o), w_r.at[w_index(o)])
        if n == 0:
            for t in (1, -1, 2, -2):
                w_push(0, t)
        elif n < 4:
            for o in W_GOT[n]:
                if o != 6:
                    w_push(o, 2 if o < 0 else -2)

    def x_push(o, carry):
        xx, yy = lax.rem(x + lax.div(o, 4), 4), lax.rem(y + lax.rem(o, 4), 4)
        send(xs.at[xx * 4 + yy], xall.at[p, c], x_s, x_r, plane(xx, yy))
        return carry

    def at(first, o1, o2):
        if first == 0:
            return lax.rem(x + o1 + 4, 4), lax.rem(y + o2 + 4, 4)
        return lax.rem(x + o2 + 4, 4), lax.rem(y + o1 + 4, 4)

    def one(rel, r, o):
        xx, yy = at(r, o, 0)
        return cot.at[rel, xx, yy, pl.ds(48 * r, 48)]

    def line(rel, r, o):
        xx, yy = at(r, 0, o)
        if r == 0:
            return cot.at[rel, pl.ds(0, 4), yy, pl.ds(0, 48)]
        return cot.at[rel, xx, pl.ds(0, 4), pl.ds(48, 48)]

    def push(ref, rel, r, k, o1, o2):
        send(ref, ref, c_s.at[rel, r, k], c_r.at[rel, r, k], plane(*at(r, o1, o2)))

    def stage(i, st):
        rel, direct = ORDER[i], i == 3
        if st == 0 and not rel:
            own_copy.wait()
        for r in range(2):
            d = 1 if (i + r) % 2 == 0 else -1
            kd, ko = (3, 4) if d == 1 else (4, 3)
            got = lambda ref, k: wait(ref, c_r.at[rel, r, k])
            if st == 0:
                if rel:
                    wait(one(rel, r, 0), za_r.at[rel - 1, r])
                push(one(rel, r, 0), rel, r, 2, 2, 0)
                push(one(rel, r, 0), rel, r, 0, 1, 0)
                push(one(rel, r, 0), rel, r, 1, -1, 0)
            elif st == 1:
                got(one(rel, r, -1), 0)
                got(one(rel, r, 1), 1)
                got(one(rel, r, 2), 2)
                if direct:
                    push(line(rel, r, 0), rel, r, 5, 0, 2)
                push(line(rel, r, 0), rel, r, 3, 0, 1)
                push(line(rel, r, 0), rel, r, 4, 0, -1)
            elif st == 2:
                got(line(rel, r, -d), kd)
                if not direct:
                    push(line(rel, r, -d), rel, r, 5, 0, d)
            else:
                got(line(rel, r, d), ko)
                got(line(rel, r, 2), 5)

    def grads(rel):
        block = cot[rel].reshape(1536, 256)
        gs[rel] = jnp.dot(xt[...], block, preferred_element_type=F32).astype(BF16).reshape(4, 64, 256)
        for t in range(1, 4):
            there = lax.rem(zl + t, 4)
            send(gs.at[rel, there], gr.at[rel, t - 1], g_s.at[rel], g_r.at[rel], (p * 4 + there, nd))

    def near_sum(rel):
        wait(gr.at[rel], g_r.at[rel])
        total = gs[rel, zl].astype(F32)
        for t in range(3):
            total = total + gr[rel, t].astype(F32)
        if rel:
            ss[rel - 1] = total.astype(BF16)
            there = lax.rem(zh + rel, 4)
            send(ss.at[rel - 1], sr.at[rel - 1], q_s.at[rel - 1], q_r.at[rel - 1], (fs, there * 2 + c))
        else:
            s_own[...] = total

    def times_w(rel, xi):
        head = wbuf[pl.ds(lax.rem(zh + rel, 4) * 4, 4)].reshape(256, 256)
        block = cot[rel, xi].reshape(384, 256)
        return lax.dot_general(block, head, (((1,), (1,)), ((), ())), preferred_element_type=F32)

    gain_here = gain_row[:, pl.ds(pl.multiple_of(p * 256, 256), 256)]

    w_round(0)
    share(1)
    share(3)
    stage(0, 0)
    share(2)
    stage(0, 1)
    lax.fori_loop(1, 16, x_push, 0)
    w_round(1)
    stage(1, 0)
    stage(2, 0)
    stage(0, 2)
    w_round(2)
    stage(1, 1)
    stage(2, 1)
    stage(3, 0)
    stage(0, 3)
    wait(xall.at[pl.ds(0, 15), 0], x_r)
    send(xall.at[pl.ds(0, 16), c], xall.at[pl.ds(0, 16), c], xb_s, xb_r, sibling)
    w_round(3)
    stage(1, 2)
    stage(2, 2)
    stage(3, 1)
    wait(xall.at[pl.ds(0, 16), 1 - c], xb_r)
    for q in range(16):
        xn[pl.ds(96 * q, 96)] = (xall[q].reshape(96, 256).astype(F32) * gain_here).astype(BF16)
    for q in range(12):
        xt[:, 128 * q : 128 * (q + 1)] = xn[128 * q : 128 * (q + 1)].T
    grads(ORDER[0])
    stage(1, 3)
    grads(ORDER[1])
    stage(2, 3)
    grads(ORDER[2])
    w_round(4)

    def three(xi, carry):
        total = times_w(ORDER[0], xi) + times_w(ORDER[1], xi) + times_w(ORDER[2], xi)
        dn[pl.ds(4 * xi, 4)] = total.reshape(4, 2, 48, 256)
        return carry

    lax.fori_loop(0, 4, three, 0)
    stage(3, 2)
    stage(3, 3)

    def last(j, gain_sum):
        xi = lax.rem(x + j + 2, 4)
        mine = pl.ds(4 * xi, 4)
        total = dn[mine] + times_w(ORDER[3], xi).reshape(4, 2, 48, 256)
        dn[mine] = total
        dsend[mine] = dn[mine, 1 - c].astype(BF16)
        send(dsend.at[mine], drecv.at[mine], e_s.at[j], e_r.at[j], sibling)
        products = (total * xall[mine].astype(F32)).reshape(384, 256)
        return gain_sum + jnp.sum(products, axis=0, keepdims=True)

    g_z[z * 2 + c] = lax.fori_loop(0, 4, last, jnp.zeros((1, 256), F32))

    def g_push(o, carry):
        send(g_z.at[z * 2 + c], g_z.at[z * 2 + c], gz_s, gz_r, column_any(lax.rem(o + 15, 32)))
        return carry

    lax.fori_loop(0, 17, g_push, 0)
    lax.fori_loop(18, 32, g_push, 0)
    grads(ORDER[3])

    def turn(j, carry):
        xi = lax.rem(x + j + 2, 4)
        mine = pl.ds(4 * xi, 4)
        wait(drecv.at[mine], e_r.at[j])
        dout[mine] = (dn[mine, c] + drecv[mine].astype(F32)).astype(BF16)

        def spread(o, inner):
            yy = lax.rem(y + o + 2, 4)

            @pl.when(lax.rem(j + 2, 4) * 4 + lax.rem(o + 2, 4) > 0)
            def _():
                send(dout.at[xi * 4 + yy], din.at[p], a_s, a_r, plane(xi, yy))

            return inner

        return lax.fori_loop(0, 4, spread, carry)

    lax.fori_loop(0, 4, turn, 0)
    din[p] = dout[p]

    near_sum(ORDER[1])
    near_sum(ORDER[2])
    near_sum(ORDER[3])
    near_sum(ORDER[0])

    wait(g_z.at[pl.ds(0, 31)], gz_r)
    g_xy[p] = jnp.sum(g_z[...], axis=0)

    def g_spread(o, carry):
        xx, yy = lax.rem(x + lax.div(o, 4), 4), lax.rem(y + lax.rem(o, 4), 4)
        send(g_xy.at[p], g_xy.at[p], gx_s, gx_r, plane(xx, yy))
        return carry

    lax.fori_loop(1, 16, g_spread, 0)

    for t in range(3):
        for r in range(2):
            wait(one(0, r, 0), za_s.at[t, r])
    for s in range(15):
        wait(wbuf.at[0], w_s.at[s])
    wait(xs.at[pl.ds(0, 15)], x_s)
    wait(xall.at[pl.ds(0, 16), 0], xb_s)
    for rel in range(4):
        for r in range(2):
            for k in range(6):
                wait(one(rel, r, 0) if k < 3 else line(rel, r, 0), c_s.at[rel, r, k])
        wait(gr.at[rel], g_s.at[rel])
        wait(dsend.at[pl.ds(0, 4)], e_s.at[rel])

    wait(din.at[pl.ds(0, 15)], a_r)
    gain_all = gain_row[...]
    for b in range(3):
        part = pl.ds(16 * b, 16)
        d = jnp.concatenate([din[q, part] for q in range(16)], axis=1).astype(F32)
        scaled = gain_all * d
        hat = xhat[part]
        stat = jnp.mean(scaled * hat, axis=-1, keepdims=True)
        dt_ref[part] = (root[part, 0:1] * (scaled - hat * stat)).astype(BF16)

    total = s_own[...]
    for k in range(3):
        wait(sr.at[k], q_r.at[k])
        total = total + sr[k].astype(F32)
    wg_ref[...] = total

    wait(g_xy.at[pl.ds(0, 15)], gx_r)
    gg_ref[...] = g_xy[...]

    for t in range(3):
        wait(ss.at[t], q_s.at[t])
    wait(dout.at[pl.ds(0, 15)], a_s)
    wait(g_z.at[pl.ds(0, 31)], gz_s)
    wait(g_xy.at[pl.ds(0, 15)], gx_s)


def local(tokens, norm_gain, kv_cotangent, weight_codes, block_scales):
    vmem, dma = pltpu.VMEM, pltpu.SemaphoreType.DMA
    hbm_spec, vmem_spec = pl.BlockSpec(memory_space=pltpu.HBM), pl.BlockSpec(memory_space=pltpu.VMEM)
    d_tokens, gain_grad, grads = pl.pallas_call(
        kernel,
        out_shape=(
            jax.ShapeDtypeStruct((48, 4096), BF16),
            jax.ShapeDtypeStruct((16, 1, 256), F32),
            jax.ShapeDtypeStruct((64, 256), F32),
        ),
        in_specs=[hbm_spec] * 5,
        out_specs=[vmem_spec] * 3,
        scratch_shapes=[
            vmem((4096,), BF16),
            vmem((1, 4096), F32),
            vmem((1, 64, 256), BF16),
            vmem((1, 64), BF16),
            vmem((4, 4, 4, 96, 256), BF16),
            vmem((16, 64, 256), BF16),
            vmem((48, 4096), BF16),
            vmem((48, 4096), F32),
            vmem((48, 128), F32),
            vmem((16, 48, 256), BF16),
            vmem((16, 2, 48, 256), BF16),
            vmem((1536, 256), BF16),
            vmem((256, 1536), BF16),
            vmem((16, 2, 48, 256), F32),
            vmem((16, 48, 256), BF16),
            vmem((16, 48, 256), BF16),
            vmem((16, 48, 256), BF16),
            vmem((16, 48, 256), BF16),
            vmem((4, 4, 64, 256), BF16),
            vmem((4, 3, 64, 256), BF16),
            vmem((64, 256), F32),
            vmem((3, 64, 256), BF16),
            vmem((3, 64, 256), BF16),
            vmem((32, 1, 256), F32),
            vmem((16, 1, 256), F32),
            dma, dma, dma, dma, dma,
            dma((3, 2)), dma((3, 2)),
            dma((15,)), dma((15,)),
            dma, dma, dma, dma,
            dma((4, 2, 6)), dma((4, 2, 6)),
            dma((4,)), dma((4,)),
            dma((3,)), dma((3,)),
            dma((4,)), dma((4,)),
            dma, dma, dma, dma, dma, dma,
        ],
        compiler_params=pltpu.CompilerParams(
            collective_id=0, has_side_effects=True, vmem_limit_bytes=52 * 1024 * 1024
        ),
    )(*[pltpu.with_memory_space_constraint(a, pltpu.HBM) for a in (tokens, norm_gain, kv_cotangent, weight_codes, block_scales)])
    return d_tokens, gain_grad.reshape(4096), grads.reshape(1, 64, 256)


def solution(mesh):
    placed = (P("fsdp", None), P(), P("fsdp", "node"), P("node", "fsdp", None), P("node", "fsdp"))
    return jax.shard_map(
        local,
        mesh=mesh,
        in_specs=placed,
        out_specs=(P(("fsdp", "node"), None), P(), P("node", "fsdp", None)),
        check_vma=False,
    )
```

```python
import jax
import jax.numpy as jnp
from jax import lax
from jax.experimental import pallas as pl
from jax.experimental.pallas import tpu as pltpu
from jax.sharding import PartitionSpec as P

MESH = pl.DeviceIdType.MESH
F32 = jnp.float32
BF16 = jnp.bfloat16
W_GOT = ((), (-1, -2, 1, 2), (-3, -4, 3, 4), (-5, -6, 5, 6), (-7, -8, 7))
ORDER = (0, 1, 3, 2)


def kernel(
    tok_hbm, gain_hbm, kv_hbm, codes_hbm, scales_hbm,
    dt_ref, gg_ref, wg_ref,
    gain_ref, gain_row, codes_ref, scales_ref, cot, wbuf, tok_v, xhat, root, xs, xall, xn, xt,
    dn, dsend, drecv, dout, din,
    gs, gr, s_own, ss, sr,
    g_z, g_xy,
    gain_sem, code_sem, scale_sem, tok_sem, own_sem, za_s, za_r, w_s, w_r, x_s, x_r, xb_s, xb_r,
    c_s, c_r, g_s, g_r, q_s, q_r, e_s, e_r, a_s, a_r,
    gz_s, gz_r, gx_s, gx_r,
):
    fs, nd = lax.axis_index("fsdp"), lax.axis_index("node")
    zl, p = lax.rem(fs, 4), lax.div(fs, 4)
    x, y = lax.div(p, 4), lax.rem(p, 4)
    zh, c = lax.div(nd, 2), lax.rem(nd, 2)
    z = zh * 4 + zl

    def plane(xx, yy):
        return ((xx * 4 + yy) * 4 + zl, nd)

    def column(zz, core=c):
        return (p * 4 + lax.rem(zz, 4), lax.div(zz, 4) * 2 + core)

    sibling = (fs, zh * 2 + (1 - c))

    def send(src, dst, send_sem, recv_sem, device):
        pltpu.make_async_remote_copy(
            src_ref=src, dst_ref=dst, send_sem=send_sem, recv_sem=recv_sem,
            device_id=device, device_id_type=MESH,
        ).start()

    def wait(ref, sem):
        pltpu.make_async_copy(ref, ref, sem).wait()

    tok_copy = pltpu.make_async_copy(
        tok_hbm.at[pl.ds(pl.multiple_of(nd * 48, 16), 48)], tok_v, tok_sem
    )
    code_copy = pltpu.make_async_copy(codes_hbm, codes_ref, code_sem)
    scale_copy = pltpu.make_async_copy(scales_hbm, scales_ref, scale_sem)
    gain_copy = pltpu.make_async_copy(gain_hbm, gain_ref, gain_sem)
    code_copy.start()
    gain_copy.start()
    scale_copy.start()
    tok_copy.start()
    own_copy = pltpu.make_async_copy(
        kv_hbm.at[pl.ds(pl.multiple_of(zh * 96, 16), 96)], cot.at[0, x, y], own_sem
    )
    own_copy.start()

    barrier = pltpu.get_barrier_semaphore()

    def column_any(o):
        return column(lax.rem(z + lax.div(o, 2), 16), lax.rem(c + o, 2))

    def greet_column(o, carry):
        pl.semaphore_signal(barrier, inc=1, device_id=column_any(lax.rem(o + 15, 32)), device_id_type=MESH)
        return carry

    def greet_plane(o, carry):
        there = plane(lax.rem(x + lax.div(o, 4), 4), lax.rem(y + lax.rem(o, 4), 4))
        pl.semaphore_signal(barrier, inc=1, device_id=there, device_id_type=MESH)
        return carry

    lax.fori_loop(0, 17, greet_column, 0)
    lax.fori_loop(18, 32, greet_column, 0)
    lax.fori_loop(1, 16, greet_plane, 0)

    code_copy.wait()
    scale_copy.wait()
    rows = lax.broadcasted_iota(jnp.int32, (64, 64), 0)
    cols = lax.broadcasted_iota(jnp.int32, (64, 64), 1)
    scales = jnp.broadcast_to(scales_ref[...].astype(F32), (64, 64))
    diagonal = jnp.where(rows == cols, scales, 0.0).astype(BF16)
    wbuf[z] = jnp.dot(diagonal, codes_ref[0], preferred_element_type=F32).astype(BF16)

    tok_copy.wait()
    for b in range(3):
        part = pl.ds(16 * b, 16)
        t = tok_v[part].astype(F32)
        inv = lax.rsqrt(jnp.mean(t * t, axis=-1, keepdims=True) + 1e-05)
        hat = t * inv
        xhat[part] = hat
        root[part] = jnp.broadcast_to(inv, (16, 128))
        for q in range(16):
            xs[q, part] = hat[:, 256 * q : 256 * (q + 1)].astype(BF16)
    xall[p, c] = xs[p]

    gain_copy.wait()
    gain_row[...] = gain_ref[...].astype(F32).reshape(1, 4096)

    pl.semaphore_wait(barrier, 46)

    def share(t):
        there = lax.rem(zh + t, 4)
        slot = (4 - t) % 4
        for r in range(2):
            send(
                kv_hbm.at[pl.ds(pl.multiple_of(there * 96 + 48 * r, 16), 48)],
                cot.at[slot, x, y, pl.ds(48 * r, 48)],
                za_s.at[t - 1, r], za_r.at[slot - 1, r], (fs, there * 2 + c),
            )

    def w_slot(o):
        return wbuf.at[lax.rem(z + o + 16, 16)]

    def w_index(o):
        return -o - 1 if o < 0 else 7 + o

    def w_push(o, t):
        k = w_index(o - t)
        send(w_slot(o), w_slot(o), w_s.at[k], w_r.at[k], column(lax.rem(z + t + 16, 16)))

    def w_round(n):
        for o in W_GOT[n]:
            wait(w_slot(o), w_r.at[w_index(o)])
        if n == 0:
            for t in (1, -1, 2, -2):
                w_push(0, t)
        elif n < 4:
            for o in W_GOT[n]:
                if o != 6:
                    w_push(o, 2 if o < 0 else -2)

    def x_push(o, carry):
        xx, yy = lax.rem(x + lax.div(o, 4), 4), lax.rem(y + lax.rem(o, 4), 4)
        send(xs.at[xx * 4 + yy], xall.at[p, c], x_s, x_r, plane(xx, yy))
        return carry

    def at(first, o1, o2):
        if first == 0:
            return lax.rem(x + o1 + 4, 4), lax.rem(y + o2 + 4, 4)
        return lax.rem(x + o2 + 4, 4), lax.rem(y + o1 + 4, 4)

    def one(rel, r, o):
        xx, yy = at(r, o, 0)
        return cot.at[rel, xx, yy, pl.ds(48 * r, 48)]

    def line(rel, r, o):
        xx, yy = at(r, 0, o)
        if r == 0:
            return cot.at[rel, pl.ds(0, 4), yy, pl.ds(0, 48)]
        return cot.at[rel, xx, pl.ds(0, 4), pl.ds(48, 48)]

    def push(ref, rel, r, k, o1, o2):
        send(ref, ref, c_s.at[rel, r, k], c_r.at[rel, r, k], plane(*at(r, o1, o2)))

    def stage(i, st):
        rel, direct = ORDER[i], i == 3
        if st == 0 and not rel:
            own_copy.wait()
        for r in range(2):
            d = 1 if (i + r) % 2 == 0 else -1
            kd, ko = (3, 4) if d == 1 else (4, 3)
            got = lambda ref, k: wait(ref, c_r.at[rel, r, k])
            if st == 0:
                if rel:
                    wait(one(rel, r, 0), za_r.at[rel - 1, r])
                push(one(rel, r, 0), rel, r, 2, 2, 0)
                push(one(rel, r, 0), rel, r, 0, 1, 0)
                push(one(rel, r, 0), rel, r, 1, -1, 0)
            elif st == 1:
                got(one(rel, r, -1), 0)
                got(one(rel, r, 1), 1)
                got(one(rel, r, 2), 2)
                if direct:
                    push(line(rel, r, 0), rel, r, 5, 0, 2)
                push(line(rel, r, 0), rel, r, 3, 0, 1)
                push(line(rel, r, 0), rel, r, 4, 0, -1)
            elif st == 2:
                got(line(rel, r, -d), kd)
                if not direct:
                    push(line(rel, r, -d), rel, r, 5, 0, d)
            else:
                got(line(rel, r, d), ko)
                got(line(rel, r, 2), 5)

    def grads(rel):
        block = cot[rel].reshape(1536, 256)
        gs[rel] = jnp.dot(xt[...], block, preferred_element_type=F32).astype(BF16).reshape(4, 64, 256)
        for t in range(1, 4):
            there = lax.rem(zl + t, 4)
            send(gs.at[rel, there], gr.at[rel, t - 1], g_s.at[rel], g_r.at[rel], (p * 4 + there, nd))

    def near_sum(rel):
        wait(gr.at[rel], g_r.at[rel])
        total = gs[rel, zl].astype(F32)
        for t in range(3):
            total = total + gr[rel, t].astype(F32)
        if rel:
            ss[rel - 1] = total.astype(BF16)
            there = lax.rem(zh + rel, 4)
            send(ss.at[rel - 1], sr.at[rel - 1], q_s.at[rel - 1], q_r.at[rel - 1], (fs, there * 2 + c))
        else:
            s_own[...] = total

    def times_w(rel, xi):
        head = wbuf[pl.ds(lax.rem(zh + rel, 4) * 4, 4)].reshape(256, 256)
        block = cot[rel, xi].reshape(384, 256)
        return lax.dot_general(block, head, (((1,), (1,)), ((), ())), preferred_element_type=F32)

    gain_here = gain_row[:, pl.ds(pl.multiple_of(p * 256, 256), 256)]

    w_round(0)
    share(1)
    share(3)
    stage(0, 0)
    share(2)
    lax.fori_loop(1, 16, x_push, 0)
    stage(0, 1)
    w_round(1)
    stage(1, 0)
    stage(2, 0)
    stage(0, 2)
    w_round(2)
    stage(1, 1)
    stage(2, 1)
    stage(3, 0)
    stage(0, 3)
    wait(xall.at[pl.ds(0, 15), 0], x_r)
    send(xall.at[pl.ds(0, 16), c], xall.at[pl.ds(0, 16), c], xb_s, xb_r, sibling)
    w_round(3)
    stage(1, 2)
    stage(2, 2)
    stage(3, 1)
    wait(xall.at[pl.ds(0, 16), 1 - c], xb_r)
    for q in range(16):
        xn[pl.ds(96 * q, 96)] = (xall[q].reshape(96, 256).astype(F32) * gain_here).astype(BF16)
    for q in range(12):
        xt[:, 128 * q : 128 * (q + 1)] = xn[128 * q : 128 * (q + 1)].T
    grads(ORDER[0])
    stage(1, 3)
    grads(ORDER[1])
    stage(2, 3)
    grads(ORDER[2])
    w_round(4)

    def three(xi, carry):
        total = times_w(ORDER[0], xi) + times_w(ORDER[1], xi) + times_w(ORDER[2], xi)
        dn[pl.ds(4 * xi, 4)] = total.reshape(4, 2, 48, 256)
        return carry

    lax.fori_loop(0, 4, three, 0)
    stage(3, 2)
    stage(3, 3)

    def last(j, gain_sum):
        xi = lax.rem(x + j, 4)
        mine = pl.ds(4 * xi, 4)
        total = dn[mine] + times_w(ORDER[3], xi).reshape(4, 2, 48, 256)
        dn[mine] = total
        dsend[mine] = dn[mine, 1 - c].astype(BF16)
        send(dsend.at[mine], drecv.at[mine], e_s.at[j], e_r.at[j], sibling)
        products = (total * xall[mine].astype(F32)).reshape(384, 256)
        return gain_sum + jnp.sum(products, axis=0, keepdims=True)

    g_z[z * 2 + c] = lax.fori_loop(0, 4, last, jnp.zeros((1, 256), F32))

    def g_push(o, carry):
        send(g_z.at[z * 2 + c], g_z.at[z * 2 + c], gz_s, gz_r, column_any(lax.rem(o + 15, 32)))
        return carry

    lax.fori_loop(0, 17, g_push, 0)
    lax.fori_loop(18, 32, g_push, 0)
    grads(ORDER[3])

    def turn(j, carry):
        xi = lax.rem(x + j, 4)
        mine = pl.ds(4 * xi, 4)
        wait(drecv.at[mine], e_r.at[j])
        dout[mine] = (dn[mine, c] + drecv[mine].astype(F32)).astype(BF16)

        def spread(o, inner):
            yy = lax.rem(y + o, 4)

            @pl.when(j * 4 + o > 0)
            def _():
                send(dout.at[xi * 4 + yy], din.at[p], a_s, a_r, plane(xi, yy))

            return inner

        return lax.fori_loop(0, 4, spread, carry)

    lax.fori_loop(0, 4, turn, 0)
    din[p] = dout[p]

    near_sum(ORDER[1])
    near_sum(ORDER[2])
    near_sum(ORDER[3])

    wait(g_z.at[pl.ds(0, 31)], gz_r)
    g_xy[p] = jnp.sum(g_z[...], axis=0)

    def g_spread(o, carry):
        xx, yy = lax.rem(x + lax.div(o, 4), 4), lax.rem(y + lax.rem(o, 4), 4)
        send(g_xy.at[p], g_xy.at[p], gx_s, gx_r, plane(xx, yy))
        return carry

    lax.fori_loop(1, 16, g_spread, 0)
    near_sum(ORDER[0])

    wait(din.at[pl.ds(0, 15)], a_r)
    gain_all = gain_row[...]
    for b in range(3):
        part = pl.ds(16 * b, 16)
        d = jnp.concatenate([din[q, part] for q in range(16)], axis=1).astype(F32)
        scaled = gain_all * d
        hat = xhat[part]
        stat = jnp.mean(scaled * hat, axis=-1, keepdims=True)
        dt_ref[part] = (root[part, 0:1] * (scaled - hat * stat)).astype(BF16)

    total = s_own[...]
    for k in range(3):
        wait(sr.at[k], q_r.at[k])
        total = total + sr[k].astype(F32)
    wg_ref[...] = total

    wait(g_xy.at[pl.ds(0, 15)], gx_r)
    gg_ref[...] = g_xy[...]

    for t in range(3):
        for r in range(2):
            wait(one(0, r, 0), za_s.at[t, r])
        wait(ss.at[t], q_s.at[t])
    for s in range(15):
        wait(wbuf.at[0], w_s.at[s])
    wait(xs.at[pl.ds(0, 15)], x_s)
    wait(xall.at[pl.ds(0, 16), 0], xb_s)
    for rel in range(4):
        for r in range(2):
            for k in range(6):
                wait(one(rel, r, 0) if k < 3 else line(rel, r, 0), c_s.at[rel, r, k])
        wait(gr.at[rel], g_s.at[rel])
        wait(dsend.at[pl.ds(0, 4)], e_s.at[rel])
    wait(dout.at[pl.ds(0, 15)], a_s)
    wait(g_z.at[pl.ds(0, 31)], gz_s)
    wait(g_xy.at[pl.ds(0, 15)], gx_s)


def local(tokens, norm_gain, kv_cotangent, weight_codes, block_scales):
    vmem, dma = pltpu.VMEM, pltpu.SemaphoreType.DMA
    hbm_spec, vmem_spec = pl.BlockSpec(memory_space=pltpu.HBM), pl.BlockSpec(memory_space=pltpu.VMEM)
    d_tokens, gain_grad, grads = pl.pallas_call(
        kernel,
        out_shape=(
            jax.ShapeDtypeStruct((48, 4096), BF16),
            jax.ShapeDtypeStruct((16, 1, 256), F32),
            jax.ShapeDtypeStruct((64, 256), F32),
        ),
        in_specs=[hbm_spec] * 5,
        out_specs=[vmem_spec] * 3,
        scratch_shapes=[
            vmem((4096,), BF16),
            vmem((1, 4096), F32),
            vmem((1, 64, 256), BF16),
            vmem((1, 64), BF16),
            vmem((4, 4, 4, 96, 256), BF16),
            vmem((16, 64, 256), BF16),
            vmem((48, 4096), BF16),
            vmem((48, 4096), F32),
            vmem((48, 128), F32),
            vmem((16, 48, 256), BF16),
            vmem((16, 2, 48, 256), BF16),
            vmem((1536, 256), BF16),
            vmem((256, 1536), BF16),
            vmem((16, 2, 48, 256), F32),
            vmem((16, 48, 256), BF16),
            vmem((16, 48, 256), BF16),
            vmem((16, 48, 256), BF16),
            vmem((16, 48, 256), BF16),
            vmem((4, 4, 64, 256), BF16),
            vmem((4, 3, 64, 256), BF16),
            vmem((64, 256), F32),
            vmem((3, 64, 256), BF16),
            vmem((3, 64, 256), BF16),
            vmem((32, 1, 256), F32),
            vmem((16, 1, 256), F32),
            dma, dma, dma, dma, dma,
            dma((3, 2)), dma((3, 2)),
            dma((15,)), dma((15,)),
            dma, dma, dma, dma,
            dma((4, 2, 6)), dma((4, 2, 6)),
            dma((4,)), dma((4,)),
            dma((3,)), dma((3,)),
            dma((4,)), dma((4,)),
            dma, dma, dma, dma, dma, dma,
        ],
        compiler_params=pltpu.CompilerParams(
            collective_id=0, has_side_effects=True, vmem_limit_bytes=52 * 1024 * 1024
        ),
    )(*[pltpu.with_memory_space_constraint(a, pltpu.HBM) for a in (tokens, norm_gain, kv_cotangent, weight_codes, block_scales)])
    return d_tokens, gain_grad.reshape(4096), grads.reshape(1, 64, 256)


def solution(mesh):
    placed = (P("fsdp", None), P(), P("fsdp", "node"), P("node", "fsdp", None), P("node", "fsdp"))
    return jax.shard_map(
        local,
        mesh=mesh,
        in_specs=placed,
        out_specs=(P(("fsdp", "node"), None), P(), P("node", "fsdp", None)),
        check_vma=False,
    )
```
